128 devices in a mesh: tile: 8 (over z, x_hi), head: 8 (over y, x_lo), dp: 2 (over core).
Axes of the slice: x: 4 (x_hi: 2, x_lo: 2; x = x_hi * 2 + x_lo), y: 4, z: 4, core: 2. Of those that a mesh axis runs over, the one named last changes fastest.
Arguments:
- queries: bfloat16 [2, 12288, 3072], P('dp', ('tile', 'head')), may hold values from -24 to 24
- keys: bfloat16 [2, 12288, 3072], P('dp', ('tile', 'head')), may hold values from -24 to 24
- values: bfloat16 [2, 12288, 3072], P('dp', ('tile', 'head')), may hold values from -6 to 6
- grad_out: bfloat16 [2, 12288, 3072], P('dp', ('tile', 'head')), may hold values from -6 to 6
- neighbours: int32 [2, 32, 4], P('dp'), may hold values from -1 to 31, as said below
Outputs:
- attended: bfloat16 [2, 12288, 3072], P('dp', ('tile', 'head'))
- grad_queries: bfloat16 [2, 12288, 3072], P('dp', ('tile', 'head'))
- grad_keys: bfloat16 [2, 12288, 3072], P('dp', ('tile', 'head'))
- grad_values: bfloat16 [2, 12288, 3072], P('dp', ('tile', 'head'))
The draws below stay inside these ranges and needn't reach their ends.
Inputs may be any that keep to these rules, and one draw needn't show every extreme that they name: `neighbours`: entry 0 of each list is the query tile itself. The other entries are distinct tiles other than it, each in the same block of 4 tiles as the query tile or in a block right beside it, followed by -1 for unused slots; each list has between 2 and 4 used entries.
All inputs are finite; a program needn't handle non-finite values.
Results may differ from the reference program's by a relative error of at most 0.029.
Values may be sent and summed in bfloat16 or wider, within the bound.
A program may use at most 128 MiB of HBM per device.

```python
import jax
import jax.numpy as jnp
from jax import lax

HEADS = 24
HD = 128
TILE = 384
NBR = 4
CLIPS = 2
TILES_DEV = 4
NTILES = 32
TOKENS = 12288


def draw_queries(key, part):
    key = jax.random.fold_in(key, 1)
    drawn = jax.random.truncated_normal(key, -6.0, 6.0, (CLIPS, TOKENS, HEADS * HD), jnp.float32)
    return drawn.astype(jnp.bfloat16)


def draw_keys(key, part):
    key = jax.random.fold_in(key, 2)
    drawn = jax.random.truncated_normal(key, -6.0, 6.0, (CLIPS, TOKENS, HEADS * HD), jnp.float32)
    return drawn.astype(jnp.bfloat16)


def draw_neighbours(key, part):
    key = jax.random.fold_in(key, 11)
    tile_ids = jnp.arange(NTILES, dtype=jnp.int32)
    blocks = tile_ids // TILES_DEV
    near = (jnp.abs(blocks[:, None] - blocks[None, :]) <= 1) & (tile_ids[:, None] != tile_ids[None, :])
    scores = jax.random.randint(jax.random.fold_in(key, 1), (CLIPS, NTILES, NTILES), 0, 2 ** 20, jnp.int32) * NTILES + tile_ids[None, None, :]
    scores = jnp.where(near[None], scores, -1)
    best, picks = jax.lax.top_k(scores, NBR - 1)
    counts = jax.random.randint(jax.random.fold_in(key, 2), (CLIPS, NTILES, 1), 1, NBR, jnp.int32)
    counts = jnp.where(tile_ids[None, :, None] == 0, 1, counts)
    slots = jnp.arange(NBR - 1, dtype=jnp.int32)[None, None, :]
    others = jnp.where(slots < counts, picks.astype(jnp.int32), -1)
    selfs = jnp.broadcast_to(tile_ids[None, :, None], (CLIPS, NTILES, 1))
    return jnp.concatenate([selfs, others], axis=2).astype(jnp.int32)


def shard_levels(key, shape, cuts, low, top_value):
    factor_of, own = 1.0, jax.random.fold_in(key, 6)
    for position, shards_of in cuts:
        steps = jnp.exp(jax.random.uniform(jax.random.fold_in(own, position), (shards_of,), jnp.float32, low / len(cuts), top_value / len(cuts)))
        factor_of = factor_of * jnp.repeat(steps, shape[position] // shards_of).reshape([-1 if axis == position else 1 for axis in range(len(shape))])
    return factor_of


def noise(key, dims, deviation, reach, pieces=(), kind=jnp.bfloat16):
    entries = deviation * jax.random.normal(key, dims, jnp.float32)
    if pieces:
        entries = entries * shard_levels(key, dims, pieces, -0.22, 0.18)
    return jnp.clip(entries, -reach, reach).astype(kind)


def setup_inputs(seed: int = 0) -> dict:
    arg_keys = jax.random.split(jax.random.key(seed), 6)
    return {
        "queries": draw_queries(jax.random.fold_in(arg_keys[5], 71), 0),
        "keys": draw_keys(jax.random.fold_in(arg_keys[5], 71), 0),
        "values": noise(arg_keys[2], (CLIPS, TOKENS, HEADS * HD), 1.0, 6.0, ((0, 2), (1, 64))),
        "grad_out": noise(arg_keys[3], (CLIPS, TOKENS, HEADS * HD), 1.0, 6.0, ((0, 2), (1, 64))),
        "neighbours": draw_neighbours(jax.random.fold_in(arg_keys[5], 71), 0),
    }


def combine_rims(acc):
    lower = acc[0].astype(jnp.bfloat16).astype(jnp.float32)
    upper = acc[2].astype(jnp.bfloat16).astype(jnp.float32)
    return (acc[1] + lower + upper).astype(jnp.bfloat16)


def reference(queries, keys, values, grad_out, neighbours):
    scale = HD ** -0.5
    outs_all, dq_all, dk_all, dv_all = [], [], [], []
    for clip in range(CLIPS):
        q_tiles = queries[clip].reshape(NTILES, TILE, HEADS, HD)
        k_tiles = keys[clip].reshape(NTILES, TILE, HEADS, HD)
        v_tiles = values[clip].reshape(NTILES, TILE, HEADS, HD)
        g_tiles = grad_out[clip].reshape(NTILES, TILE, HEADS, HD)
        lists = neighbours[clip]

        def step(carry, index):
            dk_acc, dv_acc = carry
            entry = lists[index]
            usable = entry >= 0
            safe = jnp.where(usable, entry, 0).astype(jnp.int32)
            relation = jnp.where(usable, index // TILES_DEV - safe // TILES_DEV + 1, 1).astype(jnp.int32)
            q_now = q_tiles[index].astype(jnp.float32)
            g_now = g_tiles[index].astype(jnp.float32)
            k_now = k_tiles[safe].astype(jnp.float32)
            v_now = v_tiles[safe].astype(jnp.float32)
            scores = jnp.einsum('qhd,nkhd->hqnk', q_now, k_now) * scale
            scores = jnp.where(usable[None, None, :, None], scores, -1e30)
            peak = jnp.max(scores, axis=(2, 3), keepdims=True)
            expo = jnp.exp(scores - peak)
            total = jnp.sum(expo, axis=(2, 3), keepdims=True)
            weight = expo / total
            probs = weight.astype(jnp.bfloat16).astype(jnp.float32)
            attended = jnp.einsum('hqnk,nkhd->qhd', probs, v_now).astype(jnp.bfloat16)
            delta = jnp.sum(g_now * attended.astype(jnp.float32), axis=-1)
            dprobs = jnp.einsum('qhd,nkhd->hqnk', g_now, v_now)
            dscores = (weight * (dprobs - delta.T[:, :, None, None]) * scale).astype(jnp.bfloat16).astype(jnp.float32)
            dq_now = jnp.einsum('hqnk,nkhd->qhd', dscores, k_now).astype(jnp.bfloat16)
            dk_part = jnp.einsum('hqnk,qhd->nkhd', dscores, q_now)
            dv_part = jnp.einsum('hqnk,qhd->nkhd', probs, g_now)
            dk_acc = dk_acc.at[relation, safe].add(dk_part)
            dv_acc = dv_acc.at[relation, safe].add(dv_part)
            return (dk_acc, dv_acc), (attended, dq_now)

        start = (jnp.zeros((3, NTILES, TILE, HEADS, HD), jnp.float32), jnp.zeros((3, NTILES, TILE, HEADS, HD), jnp.float32))
        (dk_acc, dv_acc), (attended, dq_tiles) = lax.scan(step, start, jnp.arange(NTILES, dtype=jnp.int32))
        outs_all.append(attended.reshape(TOKENS, HEADS * HD))
        dq_all.append(dq_tiles.reshape(TOKENS, HEADS * HD))
        dk_all.append(combine_rims(dk_acc).reshape(TOKENS, HEADS * HD))
        dv_all.append(combine_rims(dv_acc).reshape(TOKENS, HEADS * HD))
    return (jnp.stack(outs_all), jnp.stack(dq_all), jnp.stack(dk_all), jnp.stack(dv_all))
```

```python
import functools
import math

import jax
import jax.numpy as jnp
from jax import lax
from jax.experimental import pallas as pl
from jax.experimental.pallas import tpu as pltpu
from jax.sharding import PartitionSpec as P

HD = 128
TILE = 384
NBR = 4
TILES = 4
GROUP = 3
CHUNK = 64
MESH = pl.DeviceIdType.MESH
F32 = jnp.float32
BF16 = jnp.bfloat16
NT = (((1,), (1,)), ((), ()))
NN = (((1,), (0,)), ((), ()))
TN = (((0,), (0,)), ((), ()))


def dot(a, b, dims):
    return lax.dot_general(a, b, dims, preferred_element_type=F32)


def kernel(slabs, groups, *refs):
    args, places_ref, shares_ref, outs = refs[:4], refs[4], refs[5], refs[6:10]
    it = iter(refs[10:])

    def take(n):
        return [next(it) for _ in range(n)]

    qs, gs, ks, vs = take(GROUP), take(GROUP), take(GROUP), take(GROUP)
    os, dqs, dks, dvs = take(GROUP), take(GROUP), take(GROUP), take(GROUP)
    own_k, own_v = take(GROUP), take(GROUP)
    rim_out = [take(4) for _ in range(GROUP)]
    rim_in = [take(4) for _ in range(GROUP)]
    s_ref, e_ref, d_ref, dkc, dvc = take(5)
    (send_in, recv_in, halo_send, halo_recv, rim_send, rim_recv, send_out, recv_out) = take(8)

    tile = lax.axis_index("tile")
    group = lax.axis_index("head")
    core = lax.axis_index("dp")
    z = tile // 2
    side = tile % 2
    slab = 2 * z + core
    rows = TILES * TILE
    block = rows // groups
    has_self = core == side
    column = (2 * z + core, side)

    below, above = slab - 1, slab + 1
    low_id = (2 * (lax.max(below, 0) // 2) + side, group, lax.max(below, 0) % 2)
    high_id = (2 * (lax.min(above, slabs - 1) // 2) + side, group, lax.min(above, slabs - 1) % 2)
    has_low, has_high = slab > 0, slab < slabs - 1

    barrier = pltpu.get_barrier_semaphore()

    def greet(i, _):
        g = (group + i) % groups

        @pl.when(jnp.logical_or(jnp.logical_not(has_self), g != group))
        def _():
            pl.semaphore_signal(barrier, inc=1, device_id=(column[0], g, column[1]), device_id_type=MESH)

        return 0

    lax.fori_loop(0, groups, greet, 0)

    @pl.when(has_low)
    def _():
        pl.semaphore_signal(barrier, inc=1, device_id=low_id, device_id_type=MESH)

    @pl.when(has_high)
    def _():
        pl.semaphore_signal(barrier, inc=1, device_id=high_id, device_id_type=MESH)

    count = groups - has_self.astype(jnp.int32) + has_low.astype(jnp.int32) + has_high.astype(jnp.int32)
    pl.semaphore_wait(barrier, count)

    def spread(a, j, dst, offset):
        def step(i, _):
            g = (group + i) % groups
            src = args[a].at[0, :, pl.ds(pl.multiple_of((g * GROUP + j) * HD, HD), HD)]
            to = dst.at[offset + group * block // TILE, pl.ds(pl.multiple_of(group * block % TILE, block), block), :]
            here = jnp.logical_and(has_self, g == group)

            @pl.when(here)
            def _():
                pltpu.make_async_copy(src, to, recv_in.at[a, j]).start()

            @pl.when(jnp.logical_not(here))
            def _():
                pltpu.make_async_remote_copy(
                    src_ref=src, dst_ref=to, send_sem=send_in.at[a], recv_sem=recv_in.at[a, j],
                    device_id=(column[0], g, column[1]), device_id_type=MESH,
                ).start()

            return 0

        lax.fori_loop(0, groups, step, 0)

    def arrived(a, j, dst, offset):
        view = dst.at[pl.ds(offset, TILES)]
        pltpu.make_async_copy(view, view, recv_in.at[a, j]).wait()

    def home(a, j, src):
        def step(i, _):
            g = (group + i) % groups
            piece = src.at[g * block // TILE, pl.ds(pl.multiple_of(g * block % TILE, block), block), :]
            to = outs[a].at[0, :, pl.ds(pl.multiple_of((group * GROUP + j) * HD, HD), HD)]
            here = jnp.logical_and(has_self, g == group)

            @pl.when(here)
            def _():
                pltpu.make_async_copy(piece, to, recv_out.at[a]).start()

            @pl.when(jnp.logical_not(here))
            def _():
                pltpu.make_async_remote_copy(
                    src_ref=piece, dst_ref=to, send_sem=send_out.at[a], recv_sem=recv_out.at[a],
                    device_id=(column[0], g, column[1]), device_id_type=MESH,
                ).start()

            return 0

        lax.fori_loop(0, groups, step, 0)

    def halo(j, n, direction):
        src = (ks, vs)[n][j]
        return pltpu.make_async_remote_copy(
            src_ref=src.at[pl.ds(TILES, TILES)],
            dst_ref=src.at[pl.ds(0 if direction else 2 * TILES, TILES)],
            send_sem=halo_send.at[j, n, direction], recv_sem=halo_recv.at[j, n, direction],
            device_id=high_id if direction else low_id, device_id_type=MESH,
        )

    def rim(j, n, direction):
        return pltpu.make_async_remote_copy(
            src_ref=rim_out[j][2 * direction + n], dst_ref=rim_in[j][2 * (1 - direction) + n],
            send_sem=rim_send.at[j, n, direction], recv_sem=rim_recv.at[j, n, direction],
            device_id=high_id if direction else low_id, device_id_type=MESH,
        )

    def both(make, j, act):
        for direction in range(2):
            there = (has_low, has_high)[direction]
            source = (has_high, has_low)[direction]
            if act == "start":
                @pl.when(there)
                def _():
                    for n in range(2):
                        make(j, n, direction).start()
            elif act == "recv":
                @pl.when(source)
                def _():
                    for n in range(2):
                        make(j, n, direction).wait_recv()
            else:
                @pl.when(there)
                def _():
                    for n in range(2):
                        make(j, n, direction).wait_send()

    scale = HD ** -0.5
    to_two = scale * math.log2(math.e)

    def attend(j, a):
        starts, hides = [], []
        for s in range(NBR):
            starts.append(places_ref[a * NBR + s])
            hides.append(shares_ref[a * NBR + s])
        q = qs[j][a]
        peak = jnp.full((1, TILE), -1e30, F32)
        for s in range(NBR):
            scores = dot(ks[j][starts[s]], q, NT)
            s_ref[s * TILE:(s + 1) * TILE, :] = scores
            peak = jnp.maximum(peak, jnp.max(scores, axis=0, keepdims=True) - hides[s])
        total = jnp.zeros((1, TILE), F32)
        for s in range(NBR):
            floor = peak + hides[s]
            for c in range(0, TILE, CHUNK):
                part = slice(s * TILE + c, s * TILE + c + CHUNK)
                expo = jnp.exp2((s_ref[part, :] - floor) * to_two)
                total = total + jnp.sum(expo, axis=0, keepdims=True)
                e_ref[part, :] = expo.astype(BF16)
        inverse = 1.0 / total
        g_cols = (gs[j][a].astype(F32).T * inverse).astype(BF16)
        attended = jnp.zeros((HD, TILE), F32)
        delta = jnp.zeros((1, TILE), F32)
        for s in range(NBR):
            v = vs[j][starts[s]]
            span = slice(s * TILE, (s + 1) * TILE)
            s_ref[span, :] = dot(v, g_cols, NN)
            dvc[a * NBR + s] = dot(e_ref[span, :], g_cols, NT)
            attended = attended + dot(v, e_ref[span, :], TN)
            for c in range(0, TILE, CHUNK):
                part = slice(s * TILE + c, s * TILE + c + CHUNK)
                delta = delta + jnp.sum(e_ref[part, :].astype(F32) * s_ref[part, :], axis=0, keepdims=True)
        os[j][a] = (attended * inverse).T.astype(BF16)
        delta = delta * inverse
        grad_q = jnp.zeros((HD, TILE), F32)
        for s in range(NBR):
            for c in range(0, TILE, CHUNK):
                part = slice(s * TILE + c, s * TILE + c + CHUNK)
                d_ref[part, :] = (e_ref[part, :].astype(F32) * (s_ref[part, :] - delta)).astype(BF16)
            span = slice(s * TILE, (s + 1) * TILE)
            dkc[a * NBR + s] = dot(d_ref[span, :], q, NN) * scale
            grad_q = grad_q + dot(ks[j][starts[s]], d_ref[span, :], TN)
        dqs[j][a] = (grad_q * scale).T.astype(BF16)

    def gather(b):
        first = TILES * NBR + b * TILES
        places = [places_ref[first + a] for a in range(TILES)]
        shares = [shares_ref[first + a] for a in range(TILES)]
        k_sum = dkc[places[0]] * shares[0]
        v_sum = dvc[places[0]] * shares[0]
        for a in range(1, TILES):
            k_sum = k_sum + dkc[places[a]] * shares[a]
            v_sum = v_sum + dvc[places[a]] * shares[a]
        return k_sum, v_sum

    def collect(j):
        def lower(i, _):
            k_sum, v_sum = gather(i)
            rim_out[j][0][i] = k_sum.astype(BF16)
            rim_out[j][1][i] = v_sum.astype(BF16)
            return 0

        def upper(i, _):
            k_sum, v_sum = gather(i + 2 * TILES)
            rim_out[j][2][i] = k_sum.astype(BF16)
            rim_out[j][3][i] = v_sum.astype(BF16)
            return 0

        def own(i, _):
            k_sum, v_sum = gather(i + TILES)
            own_k[j][i] = k_sum
            own_v[j][i] = v_sum
            return 0

        lax.fori_loop(0, TILES, lower, 0)
        lax.fori_loop(0, TILES, upper, 0)
        both(rim, j, "start")
        lax.fori_loop(0, TILES, own, 0)

    def combine(j):
        both(rim, j, "recv")

        def step(i, _):
            dks[j][i] = (
                own_k[j][i] + rim_in[j][0][i].astype(F32) + rim_in[j][2][i].astype(F32)
            ).astype(BF16)
            dvs[j][i] = (
                own_v[j][i] + rim_in[j][1][i].astype(F32) + rim_in[j][3][i].astype(F32)
            ).astype(BF16)
            return 0

        lax.fori_loop(0, TILES, step, 0)
        home(2, j, dks[j])
        home(3, j, dvs[j])

    for j in range(GROUP):
        spread(1, j, ks[j], TILES)
        spread(2, j, vs[j], TILES)
    for j in range(GROUP):
        spread(0, j, qs[j], 0)
        spread(3, j, gs[j], 0)

    blank = jnp.zeros((TILES, TILE, HD), BF16)
    for there, first in ((has_low, 0), (has_high, 2)):
        @pl.when(jnp.logical_not(there))
        def _():
            for j in range(GROUP):
                rim_in[j][first][...] = blank
                rim_in[j][first + 1][...] = blank
                ks[j][first * TILES:(first + 1) * TILES] = blank
                vs[j][first * TILES:(first + 1) * TILES] = blank

    for j in range(GROUP):
        arrived(1, j, ks[j], TILES)
        arrived(2, j, vs[j], TILES)
        both(halo, j, "start")
    for j in range(GROUP):
        arrived(0, j, qs[j], 0)
        arrived(3, j, gs[j], 0)
        both(halo, j, "recv")

        def step(a, _):
            attend(j, a)
            return 0

        lax.fori_loop(0, TILES, step, 0)
        home(0, j, os[j])
        home(1, j, dqs[j])
        collect(j)
        if j > 0:
            combine(j - 1)
    combine(GROUP - 1)

    for j in range(GROUP):
        both(halo, j, "send")
        both(rim, j, "send")
    for refs4, sems in ((args, send_in), (outs, send_out)):
        for a in range(4):
            @pl.when(has_self)
            def _():
                view = refs4[a].at[:, :, pl.ds(0, (groups - 1) * GROUP * HD)]
                pltpu.make_async_copy(view, view, sems.at[a]).wait()

            @pl.when(jnp.logical_not(has_self))
            def _():
                pltpu.make_async_copy(refs4[a], refs4[a], sems.at[a]).wait()
    for a in range(4):
        pltpu.make_async_copy(outs[a], outs[a], recv_out.at[a]).wait()


def tables(lists):
    tile, core = lax.axis_index("tile"), lax.axis_index("dp")
    swapped = lax.ppermute(lists, "dp", [(0, 1), (1, 0)])
    lists = jnp.where(core == tile % 2, lists, swapped)
    slab = 2 * (tile // 2) + core
    mine = lax.dynamic_slice_in_dim(lists, TILES * slab, TILES, 0)
    used = mine >= 0
    query = jnp.arange(TILES, dtype=jnp.int32)[:, None]
    local = jnp.where(used, mine - TILES * slab + TILES, TILES + query)
    match = jnp.logical_and(used, local == jnp.arange(3 * TILES, dtype=jnp.int32)[:, None, None])
    slot = jnp.max(jnp.where(match, jnp.arange(NBR, dtype=jnp.int32), 0), axis=2)
    places = jnp.concatenate([local.reshape(-1), (slot + NBR * query.T).reshape(-1)])
    hides = jnp.where(used, 0.0, 1e30).astype(F32)
    shares = jnp.concatenate([hides.reshape(-1), jnp.any(match, axis=2).astype(F32).reshape(-1)])
    return places, shares


def body(queries, keys, values, grad_out, neighbours):
    slabs, groups = lax.axis_size("tile"), lax.axis_size("head")
    rows = TILES * TILE
    places, shares = tables(neighbours[0])
    head = pltpu.VMEM((TILES, TILE, HD), BF16)
    wide = pltpu.VMEM((3 * TILES, TILE, HD), BF16)
    total = pltpu.VMEM((TILES, TILE, HD), F32)
    dma = pltpu.SemaphoreType.DMA
    scratch = (
        [head] * (2 * GROUP) + [wide] * (2 * GROUP) + [head] * (4 * GROUP) + [total] * (2 * GROUP)
        + [head] * (8 * GROUP)
        + [
            pltpu.VMEM((NBR * TILE, TILE), F32),
            pltpu.VMEM((NBR * TILE, TILE), BF16),
            pltpu.VMEM((NBR * TILE, TILE), BF16),
            pltpu.VMEM((TILES * NBR, TILE, HD), F32),
            pltpu.VMEM((TILES * NBR, TILE, HD), F32),
            dma((4,)), dma((4, GROUP)), dma((GROUP, 2, 2)), dma((GROUP, 2, 2)), dma((GROUP, 2, 2)),
            dma((GROUP, 2, 2)), dma((4,)), dma((4,)),
        ]
    )
    anywhere = pl.BlockSpec(memory_space=pl.ANY)
    shape = jax.ShapeDtypeStruct(queries.shape, BF16)
    return tuple(pl.pallas_call(
        functools.partial(kernel, slabs, groups),
        out_shape=(shape,) * 4,
        in_specs=[anywhere] * 4 + [pl.BlockSpec(memory_space=pltpu.SMEM)] * 2,
        out_specs=(anywhere,) * 4,
        scratch_shapes=scratch,
        compiler_params=pltpu.CompilerParams(
            collective_id=0, has_side_effects=True, vmem_limit_bytes=58 * 1024 * 1024
        ),
    )(queries, keys, values, grad_out, places, shares))


def solution(mesh):
    tokens = P("dp", ("tile", "head"), None)
    return jax.shard_map(
        body,
        mesh=mesh,
        in_specs=(tokens,) * 4 + (P("dp", None, None),),
        out_specs=(tokens,) * 4,
        check_vma=False,
    )
```

```python
import functools
import math

import jax
import jax.numpy as jnp
from jax import lax
from jax.experimental import pallas as pl
from jax.experimental.pallas import tpu as pltpu
from jax.sharding import PartitionSpec as P

HD = 128
TILE = 384
NBR = 4
TILES = 4
GROUP = 3
CHUNK = 64
MESH = pl.DeviceIdType.MESH
F32 = jnp.float32
BF16 = jnp.bfloat16
NT = (((1,), (1,)), ((), ()))
NN = (((1,), (0,)), ((), ()))
TN = (((0,), (0,)), ((), ()))


def dot(a, b, dims):
    return lax.dot_general(a, b, dims, preferred_element_type=F32)


def kernel(slabs, groups, *refs):
    args, lists, outs = refs[:4], refs[4], refs[5:9]
    it = iter(refs[9:])

    def take(n):
        return [next(it) for _ in range(n)]

    qs, gs, ks, vs = take(GROUP), take(GROUP), take(GROUP), take(GROUP)
    os, dqs, dks, dvs = take(GROUP), take(GROUP), take(GROUP), take(GROUP)
    own_k, own_v = take(GROUP), take(GROUP)
    rim_out = [take(4) for _ in range(GROUP)]
    rim_in = [take(4) for _ in range(GROUP)]
    s_ref, e_ref, d_ref, dkc, dvc, lists_both, lists_here, places_ref, shares_ref = take(9)
    (send_in, recv_in, halo_send, halo_recv, rim_send, rim_recv, send_out, recv_out, list_sems) = take(9)

    tile = lax.axis_index("tile")
    group = lax.axis_index("head")
    core = lax.axis_index("dp")
    z = tile // 2
    side = tile % 2
    slab = 2 * z + core
    rows = TILES * TILE
    block = rows // groups
    has_self = core == side
    column = (2 * z + core, side)

    below, above = slab - 1, slab + 1
    low_id = (2 * (lax.max(below, 0) // 2) + side, group, lax.max(below, 0) % 2)
    high_id = (2 * (lax.min(above, slabs - 1) // 2) + side, group, lax.min(above, slabs - 1) % 2)
    has_low, has_high = slab > 0, slab < slabs - 1

    barrier = pltpu.get_barrier_semaphore()

    def greet(i, _):
        g = (group + i) % groups

        @pl.when(jnp.logical_or(jnp.logical_not(has_self), g != group))
        def _():
            pl.semaphore_signal(barrier, inc=1, device_id=(column[0], g, column[1]), device_id_type=MESH)

        return 0

    lax.fori_loop(0, groups, greet, 0)

    @pl.when(has_low)
    def _():
        pl.semaphore_signal(barrier, inc=1, device_id=low_id, device_id_type=MESH)

    @pl.when(has_high)
    def _():
        pl.semaphore_signal(barrier, inc=1, device_id=high_id, device_id_type=MESH)

    count = groups - has_self.astype(jnp.int32) + has_low.astype(jnp.int32) + has_high.astype(jnp.int32)
    pl.semaphore_wait(barrier, count)

    keep = pltpu.make_async_copy(lists, lists_both.at[core], list_sems.at[0])
    give = pltpu.make_async_remote_copy(
        src_ref=lists, dst_ref=lists_both.at[core], send_sem=list_sems.at[1], recv_sem=list_sems.at[2],
        device_id=(tile, group, 1 - core), device_id_type=MESH,
    )

    def tabulate():
        def entry(a, s):
            return lists_here[0, (TILES * slab + a) * NBR + s]

        def slots(a, _):
            for s in range(NBR):
                named = entry(a, s)
                used = named >= 0
                local = lax.min(lax.max(named - TILES * (slab - 1), 0), 3 * TILES - 1)
                places_ref[a * NBR + s] = jnp.where(used, local, TILES + a)
                shares_ref[a * NBR + s] = jnp.where(used, 0.0, 1e30).astype(F32)
            return 0

        def terms(b, _):
            for a in range(TILES):
                slot, share = jnp.int32(0), jnp.float32(0)
                for s in range(NBR):
                    match = entry(a, s) == TILES * (slab - 1) + b
                    slot = jnp.where(match, s, slot)
                    share = jnp.where(match, 1.0, share)
                places_ref[TILES * NBR + b * TILES + a] = a * NBR + slot
                shares_ref[TILES * NBR + b * TILES + a] = share
            return 0

        lax.fori_loop(0, TILES, slots, 0)
        lax.fori_loop(0, 3 * TILES, terms, 0)

    def spread(a, j, dst, offset):
        def step(i, _):
            g = (group + i) % groups
            src = args[a].at[0, :, pl.ds(pl.multiple_of((g * GROUP + j) * HD, HD), HD)]
            to = dst.at[offset + group * block // TILE, pl.ds(pl.multiple_of(group * block % TILE, block), block), :]
            here = jnp.logical_and(has_self, g == group)

            @pl.when(here)
            def _():
                pltpu.make_async_copy(src, to, recv_in.at[a, j]).start()

            @pl.when(jnp.logical_not(here))
            def _():
                pltpu.make_async_remote_copy(
                    src_ref=src, dst_ref=to, send_sem=send_in.at[a], recv_sem=recv_in.at[a, j],
                    device_id=(column[0], g, column[1]), device_id_type=MESH,
                ).start()

            return 0

        lax.fori_loop(0, groups, step, 0)

    def arrived(a, j, dst, offset):
        view = dst.at[pl.ds(offset, TILES)]
        pltpu.make_async_copy(view, view, recv_in.at[a, j]).wait()

    def home(a, j, src):
        def step(i, _):
            g = (group + i) % groups
            piece = src.at[g * block // TILE, pl.ds(pl.multiple_of(g * block % TILE, block), block), :]
            to = outs[a].at[0, :, pl.ds(pl.multiple_of((group * GROUP + j) * HD, HD), HD)]
            here = jnp.logical_and(has_self, g == group)

            @pl.when(here)
            def _():
                pltpu.make_async_copy(piece, to, recv_out.at[a]).start()

            @pl.when(jnp.logical_not(here))
            def _():
                pltpu.make_async_remote_copy(
                    src_ref=piece, dst_ref=to, send_sem=send_out.at[a], recv_sem=recv_out.at[a],
                    device_id=(column[0], g, column[1]), device_id_type=MESH,
                ).start()

            return 0

        lax.fori_loop(0, groups, step, 0)

    def halo(j, n, direction):
        src = (ks, vs)[n][j]
        return pltpu.make_async_remote_copy(
            src_ref=src.at[pl.ds(TILES, TILES)],
            dst_ref=src.at[pl.ds(0 if direction else 2 * TILES, TILES)],
            send_sem=halo_send.at[j, n, direction], recv_sem=halo_recv.at[j, n, direction],
            device_id=high_id if direction else low_id, device_id_type=MESH,
        )

    def rim(j, n, direction):
        return pltpu.make_async_remote_copy(
            src_ref=rim_out[j][2 * direction + n], dst_ref=rim_in[j][2 * (1 - direction) + n],
            send_sem=rim_send.at[j, n, direction], recv_sem=rim_recv.at[j, n, direction],
            device_id=high_id if direction else low_id, device_id_type=MESH,
        )

    def both(make, j, act):
        for direction in range(2):
            there = (has_low, has_high)[direction]
            source = (has_high, has_low)[direction]
            if act == "start":
                @pl.when(there)
                def _():
                    for n in range(2):
                        make(j, n, direction).start()
            elif act == "recv":
                @pl.when(source)
                def _():
                    for n in range(2):
                        make(j, n, direction).wait_recv()
            else:
                @pl.when(there)
                def _():
                    for n in range(2):
                        make(j, n, direction).wait_send()

    scale = HD ** -0.5
    to_two = scale * math.log2(math.e)

    def attend(j, a):
        starts, hides = [], []
        for s in range(NBR):
            starts.append(places_ref[a * NBR + s])
            hides.append(shares_ref[a * NBR + s])
        q = qs[j][a]
        peak = jnp.full((1, TILE), -1e30, F32)
        for s in range(NBR):
            scores = dot(ks[j][starts[s]], q, NT)
            s_ref[s * TILE:(s + 1) * TILE, :] = scores
            peak = jnp.maximum(peak, jnp.max(scores, axis=0, keepdims=True) - hides[s])
        total = jnp.zeros((1, TILE), F32)
        for s in range(NBR):
            floor = peak + hides[s]
            for c in range(0, TILE, CHUNK):
                part = slice(s * TILE + c, s * TILE + c + CHUNK)
                expo = jnp.exp2((s_ref[part, :] - floor) * to_two)
                total = total + jnp.sum(expo, axis=0, keepdims=True)
                e_ref[part, :] = expo.astype(BF16)
        inverse = 1.0 / total
        g_cols = (gs[j][a].astype(F32).T * inverse).astype(BF16)
        attended = jnp.zeros((HD, TILE), F32)
        delta = jnp.zeros((1, TILE), F32)
        for s in range(NBR):
            v = vs[j][starts[s]]
            span = slice(s * TILE, (s + 1) * TILE)
            s_ref[span, :] = dot(v, g_cols, NN)
            dvc[a * NBR + s] = dot(e_ref[span, :], g_cols, NT)
            attended = attended + dot(v, e_ref[span, :], TN)
            for c in range(0, TILE, CHUNK):
                part = slice(s * TILE + c, s * TILE + c + CHUNK)
                delta = delta + jnp.sum(e_ref[part, :].astype(F32) * s_ref[part, :], axis=0, keepdims=True)
        os[j][a] = (attended * inverse).T.astype(BF16)
        delta = delta * inverse
        grad_q = jnp.zeros((HD, TILE), F32)
        for s in range(NBR):
            for c in range(0, TILE, CHUNK):
                part = slice(s * TILE + c, s * TILE + c + CHUNK)
                d_ref[part, :] = (e_ref[part, :].astype(F32) * (s_ref[part, :] - delta)).astype(BF16)
            span = slice(s * TILE, (s + 1) * TILE)
            dkc[a * NBR + s] = dot(d_ref[span, :], q, NN) * scale
            grad_q = grad_q + dot(ks[j][starts[s]], d_ref[span, :], TN)
        dqs[j][a] = (grad_q * scale).T.astype(BF16)

    def gather(b):
        first = TILES * NBR + b * TILES
        places = [places_ref[first + a] for a in range(TILES)]
        shares = [shares_ref[first + a] for a in range(TILES)]
        k_sum = dkc[places[0]] * shares[0]
        v_sum = dvc[places[0]] * shares[0]
        for a in range(1, TILES):
            k_sum = k_sum + dkc[places[a]] * shares[a]
            v_sum = v_sum + dvc[places[a]] * shares[a]
        return k_sum, v_sum

    def collect(j):
        def lower(i, _):
            k_sum, v_sum = gather(i)
            rim_out[j][0][i] = k_sum.astype(BF16)
            rim_out[j][1][i] = v_sum.astype(BF16)
            return 0

        def upper(i, _):
            k_sum, v_sum = gather(i + 2 * TILES)
            rim_out[j][2][i] = k_sum.astype(BF16)
            rim_out[j][3][i] = v_sum.astype(BF16)
            return 0

        def own(i, _):
            k_sum, v_sum = gather(i + TILES)
            own_k[j][i] = k_sum
            own_v[j][i] = v_sum
            return 0

        lax.fori_loop(0, TILES, lower, 0)
        lax.fori_loop(0, TILES, upper, 0)
        both(rim, j, "start")
        lax.fori_loop(0, TILES, own, 0)

    def combine(j):
        both(rim, j, "recv")

        def step(i, _):
            dks[j][i] = (
                own_k[j][i] + rim_in[j][0][i].astype(F32) + rim_in[j][2][i].astype(F32)
            ).astype(BF16)
            dvs[j][i] = (
                own_v[j][i] + rim_in[j][1][i].astype(F32) + rim_in[j][3][i].astype(F32)
            ).astype(BF16)
            return 0

        lax.fori_loop(0, TILES, step, 0)
        home(2, j, dks[j])
        home(3, j, dvs[j])

    for j in range(GROUP):
        spread(1, j, ks[j], TILES)
        spread(2, j, vs[j], TILES)
        spread(0, j, qs[j], 0)
        spread(3, j, gs[j], 0)
        if j == 0:
            keep.start()
            give.start()

    blank = jnp.zeros((TILES, TILE, HD), BF16)
    for there, first in ((has_low, 0), (has_high, 2)):
        @pl.when(jnp.logical_not(there))
        def _():
            for j in range(GROUP):
                rim_in[j][first][...] = blank
                rim_in[j][first + 1][...] = blank
                ks[j][first * TILES:(first + 1) * TILES] = blank
                vs[j][first * TILES:(first + 1) * TILES] = blank

    keep.wait()
    give.wait()
    down = pltpu.make_async_copy(lists_both.at[side], lists_here, list_sems.at[3])
    down.start()
    down.wait()
    tabulate()

    def pass_on(j):
        arrived(1, j, ks[j], TILES)
        arrived(2, j, vs[j], TILES)
        both(halo, j, "start")

    pass_on(0)
    for j in range(GROUP):
        arrived(0, j, qs[j], 0)
        arrived(3, j, gs[j], 0)
        both(halo, j, "recv")

        def step(a, _):
            attend(j, a)

            @pl.when(a == TILES // 2)
            def _():
                if j < GROUP - 1:
                    pass_on(j + 1)
                if j > 0:
                    combine(j - 1)

            return 0

        lax.fori_loop(0, TILES, step, 0)
        home(0, j, os[j])
        home(1, j, dqs[j])
        collect(j)
    combine(GROUP - 1)

    for j in range(GROUP):
        both(halo, j, "send")
        both(rim, j, "send")
    for refs4, sems in ((args, send_in), (outs, send_out)):
        for a in range(4):
            @pl.when(has_self)
            def _():
                view = refs4[a].at[:, :, pl.ds(0, (groups - 1) * GROUP * HD)]
                pltpu.make_async_copy(view, view, sems.at[a]).wait()

            @pl.when(jnp.logical_not(has_self))
            def _():
                pltpu.make_async_copy(refs4[a], refs4[a], sems.at[a]).wait()
    for a in range(4):
        pltpu.make_async_copy(outs[a], outs[a], recv_out.at[a]).wait()


def settle(*refs):
    given, kept, held, sems = refs[:4], refs[4:8], refs[8], refs[9]
    parts = sems.shape[2]
    size = given[0].shape[1] // parts
    pairs = []
    for i in range(parts):
        for a in range(4):
            rows = pl.ds(i * size, size)
            pairs.append((
                pltpu.make_async_copy(given[a].at[0, rows, :], held.at[a, rows, :], sems.at[0, a, i]),
                pltpu.make_async_copy(held.at[a, rows, :], kept[a].at[0, rows, :], sems.at[1, a, i]),
            ))
    for into, _ in pairs:
        into.start()
    for into, out in pairs:
        into.wait()
        out.start()
    for _, out in pairs:
        out.wait()


def body(queries, keys, values, grad_out, neighbours):
    slabs, groups = lax.axis_size("tile"), lax.axis_size("head")
    rows = TILES * TILE
    lists = neighbours.reshape(-1)
    lists = jnp.pad(lists, (0, 8 * 128 - lists.shape[0])).reshape(8, 128)
    head = pltpu.VMEM((TILES, TILE, HD), BF16)
    wide = pltpu.VMEM((3 * TILES, TILE, HD), BF16)
    total = pltpu.VMEM((TILES, TILE, HD), F32)
    dma = pltpu.SemaphoreType.DMA
    scratch = (
        [head] * (2 * GROUP) + [wide] * (2 * GROUP) + [head] * (4 * GROUP) + [total] * (2 * GROUP)
        + [head] * (8 * GROUP)
        + [
            pltpu.VMEM((NBR * TILE, TILE), F32),
            pltpu.VMEM((NBR * TILE, TILE), BF16),
            pltpu.VMEM((NBR * TILE, TILE), BF16),
            pltpu.VMEM((TILES * NBR, TILE, HD), F32),
            pltpu.VMEM((TILES * NBR, TILE, HD), F32),
            pltpu.VMEM((2, 8, 128), jnp.int32),
            pltpu.SMEM((8, 128), jnp.int32),
            pltpu.SMEM((TILES * NBR + 3 * TILES * TILES,), jnp.int32),
            pltpu.SMEM((TILES * NBR + 3 * TILES * TILES,), F32),
            dma((4,)), dma((4, GROUP)), dma((GROUP, 2, 2)), dma((GROUP, 2, 2)), dma((GROUP, 2, 2)),
            dma((GROUP, 2, 2)), dma((4,)), dma((4,)), dma((4,)),
        ]
    )
    anywhere = pl.BlockSpec(memory_space=pl.ANY)
    shape = jax.ShapeDtypeStruct(queries.shape, BF16)
    results = pl.pallas_call(
        functools.partial(kernel, slabs, groups),
        out_shape=(shape,) * 4,
        in_specs=[anywhere] * 5,
        out_specs=(anywhere,) * 4,
        scratch_shapes=scratch,
        compiler_params=pltpu.CompilerParams(
            collective_id=0, has_side_effects=True, vmem_limit_bytes=58 * 1024 * 1024
        ),
    )(queries, keys, values, grad_out, lists)
    return tuple(pl.pallas_call(
        settle,
        out_shape=(shape,) * 4,
        in_specs=[anywhere] * 4,
        out_specs=(anywhere,) * 4,
        scratch_shapes=[pltpu.VMEM((4,) + queries.shape[1:], BF16), dma((2, 4, 4))],
    )(*results))


def solution(mesh):
    tokens = P("dp", ("tile", "head"), None)
    return jax.shard_map(
        body,
        mesh=mesh,
        in_specs=(tokens,) * 4 + (P("dp", None, None),),
        out_specs=(tokens,) * 4,
        check_vma=False,
    )
```

```python
import functools
import math

import jax
import jax.numpy as jnp
from jax import lax
from jax.experimental import pallas as pl
from jax.experimental.pallas import tpu as pltpu
from jax.sharding import PartitionSpec as P

HD = 128
TILE = 384
NBR = 4
TILES = 4
GROUP = 3
CHUNK = 64
MESH = pl.DeviceIdType.MESH
F32 = jnp.float32
BF16 = jnp.bfloat16
NT = (((1,), (1,)), ((), ()))
NN = (((1,), (0,)), ((), ()))
TN = (((0,), (0,)), ((), ()))


def dot(a, b, dims):
    return lax.dot_general(a, b, dims, preferred_element_type=F32)


def kernel(slabs, groups, *refs):
    args, lists, outs = refs[:4], refs[4], refs[5:9]
    it = iter(refs[9:])

    def take(n):
        return [next(it) for _ in range(n)]

    qs, gs, ks, vs = take(GROUP), take(GROUP), take(GROUP), take(GROUP)
    os, dqs, dks, dvs = take(GROUP), take(GROUP), take(GROUP), take(GROUP)
    own_k, own_v = take(GROUP), take(GROUP)
    rim_out = [take(4) for _ in range(GROUP)]
    rim_in = [take(4) for _ in range(GROUP)]
    s_ref, e_ref, d_ref, dkc, dvc, lists_both, lists_here, places_ref, shares_ref = take(9)
    (send_in, recv_in, halo_send, halo_recv, rim_send, rim_recv, send_out, recv_out, list_sems) = take(9)

    tile = lax.axis_index("tile")
    group = lax.axis_index("head")
    core = lax.axis_index("dp")
    z = tile // 2
    side = tile % 2
    slab = 2 * z + core
    rows = TILES * TILE
    block = rows // groups
    has_self = core == side
    column = (2 * z + core, side)

    below, above = slab - 1, slab + 1
    low_id = (2 * (lax.max(below, 0) // 2) + side, group, lax.max(below, 0) % 2)
    high_id = (2 * (lax.min(above, slabs - 1) // 2) + side, group, lax.min(above, slabs - 1) % 2)
    has_low, has_high = slab > 0, slab < slabs - 1

    barrier = pltpu.get_barrier_semaphore()

    def greet(i, _):
        g = (group + i) % groups

        @pl.when(jnp.logical_or(jnp.logical_not(has_self), g != group))
        def _():
            pl.semaphore_signal(barrier, inc=1, device_id=(column[0], g, column[1]), device_id_type=MESH)

        return 0

    lax.fori_loop(0, groups, greet, 0)

    @pl.when(has_low)
    def _():
        pl.semaphore_signal(barrier, inc=1, device_id=low_id, device_id_type=MESH)

    @pl.when(has_high)
    def _():
        pl.semaphore_signal(barrier, inc=1, device_id=high_id, device_id_type=MESH)

    count = groups - has_self.astype(jnp.int32) + has_low.astype(jnp.int32) + has_high.astype(jnp.int32)
    pl.semaphore_wait(barrier, count)

    keep = pltpu.make_async_copy(lists, lists_both.at[core], list_sems.at[0])
    give = pltpu.make_async_remote_copy(
        src_ref=lists, dst_ref=lists_both.at[core], send_sem=list_sems.at[1], recv_sem=list_sems.at[2],
        device_id=(tile, group, 1 - core), device_id_type=MESH,
    )

    def tabulate():
        def entry(a, s):
            return lists_here[s, TILES * slab + a]

        def slots(a, _):
            for s in range(NBR):
                named = entry(a, s)
                used = named >= 0
                local = lax.min(lax.max(named - TILES * (slab - 1), 0), 3 * TILES - 1)
                places_ref[a * NBR + s] = jnp.where(used, local, TILES + a)
                shares_ref[a * NBR + s] = jnp.where(used, 0.0, 1e30).astype(F32)
            return 0

        def terms(b, _):
            for a in range(TILES):
                slot, share = jnp.int32(0), jnp.float32(0)
                for s in range(NBR):
                    match = entry(a, s) == TILES * (slab - 1) + b
                    slot = jnp.where(match, s, slot)
                    share = jnp.where(match, 1.0, share)
                places_ref[TILES * NBR + b * TILES + a] = a * NBR + slot
                shares_ref[TILES * NBR + b * TILES + a] = share
            return 0

        lax.fori_loop(0, TILES, slots, 0)
        lax.fori_loop(0, 3 * TILES, terms, 0)

    def deliver(src, to, g, sent, landed):
        here = jnp.logical_and(has_self, g == group)

        @pl.when(here)
        def _():
            pltpu.make_async_copy(src, to, landed).start()

        @pl.when(jnp.logical_not(here))
        def _():
            pltpu.make_async_remote_copy(
                src_ref=src, dst_ref=to, send_sem=sent, recv_sem=landed,
                device_id=(column[0], g, column[1]), device_id_type=MESH,
            ).start()

    def spread(*moves):
        def step(i, _):
            for n, (a, j, dst, offset) in enumerate(moves):
                g = (group + i + n * groups // len(moves)) % groups
                src = args[a].at[0, :, pl.ds(pl.multiple_of((g * GROUP + j) * HD, HD), HD)]
                to = dst.at[offset + group * block // TILE, pl.ds(pl.multiple_of(group * block % TILE, block), block), :]
                deliver(src, to, g, send_in.at[a], recv_in.at[a, j])
            return 0

        lax.fori_loop(0, groups, step, 0)

    def arrived(a, j, dst, offset):
        view = dst.at[pl.ds(offset, TILES)]
        pltpu.make_async_copy(view, view, recv_in.at[a, j]).wait()

    def home(*moves):
        def step(i, _):
            for n, (a, j, src) in enumerate(moves):
                g = (group + i + n * groups // len(moves)) % groups
                piece = src.at[g * block // TILE, pl.ds(pl.multiple_of(g * block % TILE, block), block), :]
                to = outs[a].at[0, :, pl.ds(pl.multiple_of((group * GROUP + j) * HD, HD), HD)]
                deliver(piece, to, g, send_out.at[a], recv_out.at[a])
            return 0

        lax.fori_loop(0, groups, step, 0)

    def halo(j, n, direction):
        src = (ks, vs)[n][j]
        return pltpu.make_async_remote_copy(
            src_ref=src.at[pl.ds(TILES, TILES)],
            dst_ref=src.at[pl.ds(0 if direction else 2 * TILES, TILES)],
            send_sem=halo_send.at[j, n, direction], recv_sem=halo_recv.at[j, n, direction],
            device_id=high_id if direction else low_id, device_id_type=MESH,
        )

    def rim(j, n, direction):
        return pltpu.make_async_remote_copy(
            src_ref=rim_out[j][2 * direction + n], dst_ref=rim_in[j][2 * (1 - direction) + n],
            send_sem=rim_send.at[j, n, direction], recv_sem=rim_recv.at[j, n, direction],
            device_id=high_id if direction else low_id, device_id_type=MESH,
        )

    def both(make, j, act):
        for direction in range(2):
            there = (has_low, has_high)[direction]
            source = (has_high, has_low)[direction]
            if act == "start":
                @pl.when(there)
                def _():
                    for n in range(2):
                        make(j, n, direction).start()
            elif act == "recv":
                @pl.when(source)
                def _():
                    for n in range(2):
                        make(j, n, direction).wait_recv()
            else:
                @pl.when(there)
                def _():
                    for n in range(2):
                        make(j, n, direction).wait_send()

    scale = HD ** -0.5
    to_two = scale * math.log2(math.e)

    def attend(j, a):
        starts, hides = [], []
        for s in range(NBR):
            starts.append(places_ref[a * NBR + s])
            hides.append(shares_ref[a * NBR + s])
        q = qs[j][a]
        peak = jnp.full((1, TILE), -1e30, F32)
        for s in range(NBR):
            scores = dot(ks[j][starts[s]], q, NT)
            s_ref[s * TILE:(s + 1) * TILE, :] = scores
            peak = jnp.maximum(peak, jnp.max(scores, axis=0, keepdims=True) - hides[s])
        total = jnp.zeros((1, TILE), F32)
        for s in range(NBR):
            floor = peak + hides[s]
            for c in range(0, TILE, CHUNK):
                part = slice(s * TILE + c, s * TILE + c + CHUNK)
                expo = jnp.exp2((s_ref[part, :] - floor) * to_two)
                total = total + jnp.sum(expo, axis=0, keepdims=True)
                e_ref[part, :] = expo.astype(BF16)
        inverse = 1.0 / total
        g_cols = (gs[j][a].astype(F32).T * inverse).astype(BF16)
        attended = jnp.zeros((HD, TILE), F32)
        delta = jnp.zeros((1, TILE), F32)
        for s in range(NBR):
            v = vs[j][starts[s]]
            span = slice(s * TILE, (s + 1) * TILE)
            s_ref[span, :] = dot(v, g_cols, NN)
            dvc[a * NBR + s] = dot(e_ref[span, :], g_cols, NT)
            attended = attended + dot(v, e_ref[span, :], TN)
            for c in range(0, TILE, CHUNK):
                part = slice(s * TILE + c, s * TILE + c + CHUNK)
                delta = delta + jnp.sum(e_ref[part, :].astype(F32) * s_ref[part, :], axis=0, keepdims=True)
        os[j][a] = (attended * inverse).T.astype(BF16)
        delta = delta * inverse
        grad_q = jnp.zeros((HD, TILE), F32)
        for s in range(NBR):
            for c in range(0, TILE, CHUNK):
                part = slice(s * TILE + c, s * TILE + c + CHUNK)
                d_ref[part, :] = (e_ref[part, :].astype(F32) * (s_ref[part, :] - delta)).astype(BF16)
            span = slice(s * TILE, (s + 1) * TILE)
            dkc[a * NBR + s] = dot(d_ref[span, :], q, NN) * scale
            grad_q = grad_q + dot(ks[j][starts[s]], d_ref[span, :], TN)
        dqs[j][a] = (grad_q * scale).T.astype(BF16)

    def gather(b):
        first = TILES * NBR + b * TILES
        places = [places_ref[first + a] for a in range(TILES)]
        shares = [shares_ref[first + a] for a in range(TILES)]
        k_sum = dkc[places[0]] * shares[0]
        v_sum = dvc[places[0]] * shares[0]
        for a in range(1, TILES):
            k_sum = k_sum + dkc[places[a]] * shares[a]
            v_sum = v_sum + dvc[places[a]] * shares[a]
        return k_sum, v_sum

    def collect(j):
        def lower(i, _):
            k_sum, v_sum = gather(i)
            rim_out[j][0][i] = k_sum.astype(BF16)
            rim_out[j][1][i] = v_sum.astype(BF16)
            return 0

        def upper(i, _):
            k_sum, v_sum = gather(i + 2 * TILES)
            rim_out[j][2][i] = k_sum.astype(BF16)
            rim_out[j][3][i] = v_sum.astype(BF16)
            return 0

        def own(i, _):
            k_sum, v_sum = gather(i + TILES)
            own_k[j][i] = k_sum
            own_v[j][i] = v_sum
            return 0

        lax.fori_loop(0, TILES, lower, 0)
        lax.fori_loop(0, TILES, upper, 0)
        both(rim, j, "start")
        lax.fori_loop(0, TILES, own, 0)

    def combine(j):
        both(rim, j, "recv")

        def step(i, _):
            dks[j][i] = (
                own_k[j][i] + rim_in[j][0][i].astype(F32) + rim_in[j][2][i].astype(F32)
            ).astype(BF16)
            dvs[j][i] = (
                own_v[j][i] + rim_in[j][1][i].astype(F32) + rim_in[j][3][i].astype(F32)
            ).astype(BF16)
            return 0

        lax.fori_loop(0, TILES, step, 0)
        home((2, j, dks[j]), (3, j, dvs[j]))

    for j in range(GROUP):
        spread((1, j, ks[j], TILES), (2, j, vs[j], TILES))
        spread((0, j, qs[j], 0), (3, j, gs[j], 0))
        if j == 0:
            keep.start()
            give.start()

    blank = jnp.zeros((TILES, TILE, HD), BF16)
    for there, first in ((has_low, 0), (has_high, 2)):
        @pl.when(jnp.logical_not(there))
        def _():
            for j in range(GROUP):
                rim_in[j][first][...] = blank
                rim_in[j][first + 1][...] = blank
                ks[j][first * TILES:(first + 1) * TILES] = blank
                vs[j][first * TILES:(first + 1) * TILES] = blank

    keep.wait()
    give.wait()
    down = pltpu.make_async_copy(lists_both.at[side], lists_here, list_sems.at[3])
    down.start()
    down.wait()
    tabulate()

    def pass_on(j):
        arrived(1, j, ks[j], TILES)
        arrived(2, j, vs[j], TILES)
        both(halo, j, "start")

    pass_on(0)
    for j in range(GROUP):
        arrived(0, j, qs[j], 0)
        arrived(3, j, gs[j], 0)
        both(halo, j, "recv")

        def step(a, _):
            attend(j, a)

            @pl.when(a == TILES // 2)
            def _():
                if j < GROUP - 1:
                    pass_on(j + 1)
                if j > 0:
                    combine(j - 1)

            return 0

        lax.fori_loop(0, TILES, step, 0)
        home((0, j, os[j]), (1, j, dqs[j]))
        collect(j)
    combine(GROUP - 1)

    for j in range(GROUP):
        both(halo, j, "send")
        both(rim, j, "send")
    for refs4, sems in ((args, send_in), (outs, send_out)):
        for a in range(4):
            @pl.when(has_self)
            def _():
                view = refs4[a].at[:, :, pl.ds(0, (groups - 1) * GROUP * HD)]
                pltpu.make_async_copy(view, view, sems.at[a]).wait()

            @pl.when(jnp.logical_not(has_self))
            def _():
                pltpu.make_async_copy(refs4[a], refs4[a], sems.at[a]).wait()
    for a in range(4):
        pltpu.make_async_copy(outs[a], outs[a], recv_out.at[a]).wait()


def settle(*refs):
    given, kept, sems = refs[:4], refs[4:8], refs[8]
    parts = sems.shape[1]
    size = given[0].shape[1] // parts
    copies = []
    for i in range(parts):
        for a in range(4):
            rows = pl.ds(i * size, size)
            copies.append(pltpu.make_async_copy(given[a].at[0, rows, :], kept[a].at[0, rows, :], sems.at[a, i]))
    for copy in copies:
        copy.start()
    for copy in copies:
        copy.wait()


def body(queries, keys, values, grad_out, neighbours):
    slabs, groups = lax.axis_size("tile"), lax.axis_size("head")
    rows = TILES * TILE
    lists = neighbours[0].T
    head = pltpu.VMEM((TILES, TILE, HD), BF16)
    wide = pltpu.VMEM((3 * TILES, TILE, HD), BF16)
    total = pltpu.VMEM((TILES, TILE, HD), F32)
    dma = pltpu.SemaphoreType.DMA
    scratch = (
        [head] * (2 * GROUP) + [wide] * (2 * GROUP) + [head] * (4 * GROUP) + [total] * (2 * GROUP)
        + [head] * (8 * GROUP)
        + [
            pltpu.VMEM((NBR * TILE, TILE), F32),
            pltpu.VMEM((NBR * TILE, TILE), BF16),
            pltpu.VMEM((NBR * TILE, TILE), BF16),
            pltpu.VMEM((TILES * NBR, TILE, HD), F32),
            pltpu.VMEM((TILES * NBR, TILE, HD), F32),
            pltpu.VMEM((2,) + lists.shape, jnp.int32),
            pltpu.SMEM(lists.shape, jnp.int32),
            pltpu.SMEM((TILES * NBR + 3 * TILES * TILES,), jnp.int32),
            pltpu.SMEM((TILES * NBR + 3 * TILES * TILES,), F32),
            dma((4,)), dma((4, GROUP)), dma((GROUP, 2, 2)), dma((GROUP, 2, 2)), dma((GROUP, 2, 2)),
            dma((GROUP, 2, 2)), dma((4,)), dma((4,)), dma((4,)),
        ]
    )
    anywhere = pl.BlockSpec(memory_space=pl.ANY)
    shape = jax.ShapeDtypeStruct(queries.shape, BF16)
    results = pl.pallas_call(
        functools.partial(kernel, slabs, groups),
        out_shape=(pltpu.VMEM(queries.shape, BF16),) * 4,
        in_specs=[anywhere] * 5,
        out_specs=(anywhere,) * 4,
        scratch_shapes=scratch,
        compiler_params=pltpu.CompilerParams(
            collective_id=0, has_side_effects=True, vmem_limit_bytes=54 * 1024 * 1024
        ),
    )(*(pltpu.with_memory_space_constraint(x, pltpu.HBM) for x in (queries, keys, values, grad_out)), lists)
    results = [pltpu.with_memory_space_constraint(r, pltpu.VMEM) for r in results]
    return tuple(pl.pallas_call(
        settle,
        out_shape=(shape,) * 4,
        in_specs=[pl.BlockSpec(memory_space=pltpu.VMEM)] * 4,
        out_specs=(anywhere,) * 4,
        scratch_shapes=[dma((4, 1))],
        compiler_params=pltpu.CompilerParams(vmem_limit_bytes=4 * 1024 * 1024),
    )(*results))


def solution(mesh):
    tokens = P("dp", ("tile", "head"), None)
    return jax.shard_map(
        body,
        mesh=mesh,
        in_specs=(tokens,) * 4 + (P("dp", None, None),),
        out_specs=(tokens,) * 4,
        check_vma=False,
    )
```

```python
import functools
import math

import jax
import jax.numpy as jnp
from jax import lax
from jax.experimental import pallas as pl
from jax.experimental.pallas import tpu as pltpu
from jax.sharding import PartitionSpec as P

HD = 128
TILE = 384
NBR = 4
TILES = 4
GROUP = 3
CHUNK = 64
MESH = pl.DeviceIdType.MESH
F32 = jnp.float32
BF16 = jnp.bfloat16
NT = (((1,), (1,)), ((), ()))
NN = (((1,), (0,)), ((), ()))
TN = (((0,), (0,)), ((), ()))


def dot(a, b, dims):
    return lax.dot_general(a, b, dims, preferred_element_type=F32)


def kernel(slabs, groups, *refs):
    args, lists, outs = refs[:4], refs[4], refs[5:9]
    it = iter(refs[9:])

    def take(n):
        return [next(it) for _ in range(n)]

    qs, gs, ks, vs = take(GROUP), take(GROUP), take(GROUP), take(GROUP)
    os, dqs, dks, dvs = take(GROUP), take(GROUP), take(GROUP), take(GROUP)
    own_k, own_v = take(GROUP), take(GROUP)
    rim_out = [take(4) for _ in range(GROUP)]
    rim_in = [take(4) for _ in range(GROUP)]
    s_ref, e_ref, d_ref, dkc, dvc, lists_both, lists_here, places_ref, shares_ref = take(9)
    (send_in, recv_in, halo_send, halo_recv, rim_send, rim_recv, send_out, recv_out, list_sems) = take(9)

    tile = lax.axis_index("tile")
    group = lax.axis_index("head")
    core = lax.axis_index("dp")
    z = tile // 2
    side = tile % 2
    slab = 2 * z + core
    rows = TILES * TILE
    block = rows // groups
    has_self = core == side
    column = (2 * z + core, side)

    below, above = slab - 1, slab + 1
    low_id = (2 * (lax.max(below, 0) // 2) + side, group, lax.max(below, 0) % 2)
    high_id = (2 * (lax.min(above, slabs - 1) // 2) + side, group, lax.min(above, slabs - 1) % 2)
    has_low, has_high = slab > 0, slab < slabs - 1

    barrier = pltpu.get_barrier_semaphore()

    def greet(i, _):
        g = (group + i) % groups

        @pl.when(jnp.logical_or(jnp.logical_not(has_self), g != group))
        def _():
            pl.semaphore_signal(barrier, inc=1, device_id=(column[0], g, column[1]), device_id_type=MESH)

        return 0

    lax.fori_loop(0, groups, greet, 0)

    @pl.when(has_low)
    def _():
        pl.semaphore_signal(barrier, inc=1, device_id=low_id, device_id_type=MESH)

    @pl.when(has_high)
    def _():
        pl.semaphore_signal(barrier, inc=1, device_id=high_id, device_id_type=MESH)

    count = groups - has_self.astype(jnp.int32) + has_low.astype(jnp.int32) + has_high.astype(jnp.int32)
    pl.semaphore_wait(barrier, count)

    keep = pltpu.make_async_copy(lists, lists_both.at[core], list_sems.at[0])
    give = pltpu.make_async_remote_copy(
        src_ref=lists, dst_ref=lists_both.at[core], send_sem=list_sems.at[1], recv_sem=list_sems.at[2],
        device_id=(tile, group, 1 - core), device_id_type=MESH,
    )

    def tabulate():
        def entry(a, s):
            return lists_here[s, TILES * slab + a]

        def slots(a, _):
            for s in range(NBR):
                named = entry(a, s)
                used = named >= 0
                local = lax.min(lax.max(named - TILES * (slab - 1), 0), 3 * TILES - 1)
                places_ref[a * NBR + s] = jnp.where(used, local, TILES + a)
                shares_ref[a * NBR + s] = jnp.where(used, 0.0, 1e30).astype(F32)
            return 0

        def terms(b, _):
            for a in range(TILES):
                slot, share = jnp.int32(0), jnp.float32(0)
                for s in range(NBR):
                    match = entry(a, s) == TILES * (slab - 1) + b
                    slot = jnp.where(match, s, slot)
                    share = jnp.where(match, 1.0, share)
                places_ref[TILES * NBR + b * TILES + a] = a * NBR + slot
                shares_ref[TILES * NBR + b * TILES + a] = share
            return 0

        lax.fori_loop(0, TILES, slots, 0)
        lax.fori_loop(0, 3 * TILES, terms, 0)

    def deliver(src, to, g, sent, landed):
        here = jnp.logical_and(has_self, g == group)

        @pl.when(here)
        def _():
            pltpu.make_async_copy(src, to, landed).start()

        @pl.when(jnp.logical_not(here))
        def _():
            pltpu.make_async_remote_copy(
                src_ref=src, dst_ref=to, send_sem=sent, recv_sem=landed,
                device_id=(column[0], g, column[1]), device_id_type=MESH,
            ).start()

    def spread(*moves):
        def step(i, _):
            for n, (a, j, dst, offset) in enumerate(moves):
                g = (group + n * groups // len(moves) + i * (1 - 2 * core) + groups) % groups
                src = args[a].at[0, :, pl.ds(pl.multiple_of((g * GROUP + j) * HD, HD), HD)]
                to = dst.at[offset + group * block // TILE, pl.ds(pl.multiple_of(group * block % TILE, block), block), :]
                deliver(src, to, g, send_in.at[a], recv_in.at[a, j])
            return 0

        lax.fori_loop(0, groups, step, 0)

    def arrived(a, j, dst, offset):
        view = dst.at[pl.ds(offset, TILES)]
        pltpu.make_async_copy(view, view, recv_in.at[a, j]).wait()

    def home(*moves):
        def step(i, _):
            for n, (a, j, src) in enumerate(moves):
                g = (group + n * groups // len(moves) + i * (1 - 2 * core) + groups) % groups
                piece = src.at[g * block // TILE, pl.ds(pl.multiple_of(g * block % TILE, block), block), :]
                to = outs[a].at[0, :, pl.ds(pl.multiple_of((group * GROUP + j) * HD, HD), HD)]
                deliver(piece, to, g, send_out.at[a], recv_out.at[a])
            return 0

        lax.fori_loop(0, groups, step, 0)

    def halo(j, n, direction):
        src = (ks, vs)[n][j]
        return pltpu.make_async_remote_copy(
            src_ref=src.at[pl.ds(TILES, TILES)],
            dst_ref=src.at[pl.ds(0 if direction else 2 * TILES, TILES)],
            send_sem=halo_send.at[j, n, direction], recv_sem=halo_recv.at[j, n, direction],
            device_id=high_id if direction else low_id, device_id_type=MESH,
        )

    def rim(j, n, direction):
        return pltpu.make_async_remote_copy(
            src_ref=rim_out[j][2 * direction + n], dst_ref=rim_in[j][2 * (1 - direction) + n],
            send_sem=rim_send.at[j, n, direction], recv_sem=rim_recv.at[j, n, direction],
            device_id=high_id if direction else low_id, device_id_type=MESH,
        )

    def both(make, j, act):
        for direction in range(2):
            there = (has_low, has_high)[direction]
            source = (has_high, has_low)[direction]
            if act == "start":
                @pl.when(there)
                def _():
                    for n in range(2):
                        make(j, n, direction).start()
            elif act == "recv":
                @pl.when(source)
                def _():
                    for n in range(2):
                        make(j, n, direction).wait_recv()
            else:
                @pl.when(there)
                def _():
                    for n in range(2):
                        make(j, n, direction).wait_send()

    scale = HD ** -0.5
    to_two = scale * math.log2(math.e)

    def attend(j, a):
        starts, hides = [], []
        for s in range(NBR):
            starts.append(places_ref[a * NBR + s])
            hides.append(shares_ref[a * NBR + s])
        q = qs[j][a]
        peak = jnp.full((1, TILE), -1e30, F32)
        for s in range(NBR):
            scores = dot(ks[j][starts[s]], q, NT)
            s_ref[s * TILE:(s + 1) * TILE, :] = scores
            peak = jnp.maximum(peak, jnp.max(scores, axis=0, keepdims=True) - hides[s])
        total = jnp.zeros((1, TILE), F32)
        for s in range(NBR):
            floor = peak + hides[s]
            for c in range(0, TILE, CHUNK):
                part = slice(s * TILE + c, s * TILE + c + CHUNK)
                expo = jnp.exp2((s_ref[part, :] - floor) * to_two)
                total = total + jnp.sum(expo, axis=0, keepdims=True)
                e_ref[part, :] = expo.astype(BF16)
        inverse = 1.0 / total
        g_cols = (gs[j][a].astype(F32).T * inverse).astype(BF16)
        attended = jnp.zeros((HD, TILE), F32)
        delta = jnp.zeros((1, TILE), F32)
        for s in range(NBR):
            v = vs[j][starts[s]]
            span = slice(s * TILE, (s + 1) * TILE)
            s_ref[span, :] = dot(v, g_cols, NN)
            dvc[a * NBR + s] = dot(e_ref[span, :], g_cols, NT)
            attended = attended + dot(v, e_ref[span, :], TN)
            for c in range(0, TILE, CHUNK):
                part = slice(s * TILE + c, s * TILE + c + CHUNK)
                delta = delta + jnp.sum(e_ref[part, :].astype(F32) * s_ref[part, :], axis=0, keepdims=True)
        os[j][a] = (attended * inverse).T.astype(BF16)
        delta = delta * inverse
        grad_q = jnp.zeros((HD, TILE), F32)
        for s in range(NBR):
            for c in range(0, TILE, CHUNK):
                part = slice(s * TILE + c, s * TILE + c + CHUNK)
                d_ref[part, :] = (e_ref[part, :].astype(F32) * (s_ref[part, :] - delta)).astype(BF16)
            span = slice(s * TILE, (s + 1) * TILE)
            dkc[a * NBR + s] = dot(d_ref[span, :], q, NN) * scale
            grad_q = grad_q + dot(ks[j][starts[s]], d_ref[span, :], TN)
        dqs[j][a] = (grad_q * scale).T.astype(BF16)

    def gather(b):
        first = TILES * NBR + b * TILES
        places = [places_ref[first + a] for a in range(TILES)]
        shares = [shares_ref[first + a] for a in range(TILES)]
        k_sum = dkc[places[0]] * shares[0]
        v_sum = dvc[places[0]] * shares[0]
        for a in range(1, TILES):
            k_sum = k_sum + dkc[places[a]] * shares[a]
            v_sum = v_sum + dvc[places[a]] * shares[a]
        return k_sum, v_sum

    def collect(j):
        def lower(i, _):
            k_sum, v_sum = gather(i)
            rim_out[j][0][i] = k_sum.astype(BF16)
            rim_out[j][1][i] = v_sum.astype(BF16)
            return 0

        def upper(i, _):
            k_sum, v_sum = gather(i + 2 * TILES)
            rim_out[j][2][i] = k_sum.astype(BF16)
            rim_out[j][3][i] = v_sum.astype(BF16)
            return 0

        def own(i, _):
            k_sum, v_sum = gather(i + TILES)
            own_k[j][i] = k_sum
            own_v[j][i] = v_sum
            return 0

        lax.fori_loop(0, TILES, lower, 0)
        lax.fori_loop(0, TILES, upper, 0)
        both(rim, j, "start")
        home((0, j, os[j]), (1, j, dqs[j]))
        lax.fori_loop(0, TILES, own, 0)

    def combine(j):
        both(rim, j, "recv")

        def step(i, _):
            dks[j][i] = (
                own_k[j][i] + rim_in[j][0][i].astype(F32) + rim_in[j][2][i].astype(F32)
            ).astype(BF16)
            dvs[j][i] = (
                own_v[j][i] + rim_in[j][1][i].astype(F32) + rim_in[j][3][i].astype(F32)
            ).astype(BF16)
            return 0

        lax.fori_loop(0, TILES, step, 0)
        home((2, j, dks[j]), (3, j, dvs[j]))

    for j in range(GROUP):
        spread((1, j, ks[j], TILES), (2, j, vs[j], TILES))
        spread((0, j, qs[j], 0), (3, j, gs[j], 0))
        if j == 0:
            keep.start()
            give.start()

    blank = jnp.zeros((TILES, TILE, HD), BF16)
    for there, first in ((has_low, 0), (has_high, 2)):
        @pl.when(jnp.logical_not(there))
        def _():
            for j in range(GROUP):
                rim_in[j][first][...] = blank
                rim_in[j][first + 1][...] = blank
                ks[j][first * TILES:(first + 1) * TILES] = blank
                vs[j][first * TILES:(first + 1) * TILES] = blank

    keep.wait()
    give.wait()
    down = pltpu.make_async_copy(lists_both.at[side], lists_here, list_sems.at[3])
    down.start()
    down.wait()
    tabulate()

    def pass_on(j):
        arrived(1, j, ks[j], TILES)
        arrived(2, j, vs[j], TILES)
        both(halo, j, "start")

    pass_on(0)
    for j in range(GROUP):
        arrived(0, j, qs[j], 0)
        arrived(3, j, gs[j], 0)
        both(halo, j, "recv")

        def step(a, _):
            attend(j, a)

            @pl.when(a == TILES // 2)
            def _():
                if j < GROUP - 1:
                    pass_on(j + 1)
                if j > 0:
                    combine(j - 1)

            return 0

        lax.fori_loop(0, TILES, step, 0)
        collect(j)
    combine(GROUP - 1)

    for j in range(GROUP):
        both(halo, j, "send")
        both(rim, j, "send")
    for refs4, sems in ((args, send_in), (outs, send_out)):
        for a in range(4):
            @pl.when(has_self)
            def _():
                view = refs4[a].at[:, :, pl.ds(0, (groups - 1) * GROUP * HD)]
                pltpu.make_async_copy(view, view, sems.at[a]).wait()

            @pl.when(jnp.logical_not(has_self))
            def _():
                pltpu.make_async_copy(refs4[a], refs4[a], sems.at[a]).wait()
    for a in range(4):
        pltpu.make_async_copy(outs[a], outs[a], recv_out.at[a]).wait()


def settle(*refs):
    given, kept, sems = refs[:4], refs[4:8], refs[8]
    parts = sems.shape[1]
    size = given[0].shape[1] // parts
    copies = []
    for i in range(parts):
        for a in range(4):
            rows = pl.ds(i * size, size)
            copies.append(pltpu.make_async_copy(given[a].at[0, rows, :], kept[a].at[0, rows, :], sems.at[a, i]))
    for copy in copies:
        copy.start()
    for copy in copies:
        copy.wait()


def body(queries, keys, values, grad_out, neighbours):
    slabs, groups = lax.axis_size("tile"), lax.axis_size("head")
    rows = TILES * TILE
    lists = neighbours[0].T
    head = pltpu.VMEM((TILES, TILE, HD), BF16)
    wide = pltpu.VMEM((3 * TILES, TILE, HD), BF16)
    total = pltpu.VMEM((TILES, TILE, HD), F32)
    dma = pltpu.SemaphoreType.DMA
    scratch = (
        [head] * (2 * GROUP) + [wide] * (2 * GROUP) + [head] * (4 * GROUP) + [total] * (2 * GROUP)
        + [head] * (8 * GROUP)
        + [
            pltpu.VMEM((NBR * TILE, TILE), F32),
            pltpu.VMEM((NBR * TILE, TILE), BF16),
            pltpu.VMEM((NBR * TILE, TILE), BF16),
            pltpu.VMEM((TILES * NBR, TILE, HD), F32),
            pltpu.VMEM((TILES * NBR, TILE, HD), F32),
            pltpu.VMEM((2,) + lists.shape, jnp.int32),
            pltpu.SMEM(lists.shape, jnp.int32),
            pltpu.SMEM((TILES * NBR + 3 * TILES * TILES,), jnp.int32),
            pltpu.SMEM((TILES * NBR + 3 * TILES * TILES,), F32),
            dma((4,)), dma((4, GROUP)), dma((GROUP, 2, 2)), dma((GROUP, 2, 2)), dma((GROUP, 2, 2)),
            dma((GROUP, 2, 2)), dma((4,)), dma((4,)), dma((4,)),
        ]
    )
    anywhere = pl.BlockSpec(memory_space=pl.ANY)
    shape = jax.ShapeDtypeStruct(queries.shape, BF16)
    results = pl.pallas_call(
        functools.partial(kernel, slabs, groups),
        out_shape=(pltpu.VMEM(queries.shape, BF16),) * 4,
        in_specs=[anywhere] * 5,
        out_specs=(anywhere,) * 4,
        scratch_shapes=scratch,
        compiler_params=pltpu.CompilerParams(
            collective_id=0, has_side_effects=True, vmem_limit_bytes=54 * 1024 * 1024
        ),
    )(*(pltpu.with_memory_space_constraint(x, pltpu.HBM) for x in (queries, keys, values, grad_out)), lists)
    results = [pltpu.with_memory_space_constraint(r, pltpu.VMEM) for r in results]
    return tuple(pl.pallas_call(
        settle,
        out_shape=(shape,) * 4,
        in_specs=[pl.BlockSpec(memory_space=pltpu.VMEM)] * 4,
        out_specs=(anywhere,) * 4,
        scratch_shapes=[dma((4, 1))],
        compiler_params=pltpu.CompilerParams(vmem_limit_bytes=4 * 1024 * 1024),
    )(*results))


def solution(mesh):
    tokens = P("dp", ("tile", "head"), None)
    return jax.shard_map(
        body,
        mesh=mesh,
        in_specs=(tokens,) * 4 + (P("dp", None, None),),
        out_specs=(tokens,) * 4,
        check_vma=False,
    )
```

```python
import functools
import math

import jax
import jax.numpy as jnp
from jax import lax
from jax.experimental import pallas as pl
from jax.experimental.pallas import tpu as pltpu
from jax.sharding import PartitionSpec as P

HD = 128
TILE = 384
NBR = 4
TILES = 4
GROUP = 3
CHUNK = 64
MESH = pl.DeviceIdType.MESH
F32 = jnp.float32
BF16 = jnp.bfloat16
NT = (((1,), (1,)), ((), ()))
NN = (((1,), (0,)), ((), ()))
TN = (((0,), (0,)), ((), ()))


def dot(a, b, dims):
    return lax.dot_general(a, b, dims, preferred_element_type=F32)


def kernel(slabs, groups, *refs):
    args, lists, outs = refs[:4], refs[4], refs[5:9]
    it = iter(refs[9:])

    def take(n):
        return [next(it) for _ in range(n)]

    qs, gs, ks, vs = take(GROUP), take(GROUP), take(GROUP), take(GROUP)
    os, dqs, dks, dvs = take(GROUP), take(GROUP), take(GROUP), take(GROUP)
    own_k, own_v = take(GROUP), take(GROUP)
    rim_out = [take(4) for _ in range(GROUP)]
    rim_in = [take(4) for _ in range(GROUP)]
    s_ref, e_ref, d_ref, dkc, dvc, lists_both, lists_here, places_ref, shares_ref = take(9)
    (send_in, recv_in, halo_send, halo_recv, rim_send, rim_recv, send_out, recv_out, list_sems) = take(9)

    tile = lax.axis_index("tile")
    group = lax.axis_index("head")
    core = lax.axis_index("dp")
    z = tile // 2
    side = tile % 2
    slab = 2 * z + core
    rows = TILES * TILE
    block = rows // groups
    has_self = core == side
    column = (2 * z + core, side)

    below, above = slab - 1, slab + 1
    low_id = (2 * (lax.max(below, 0) // 2) + side, group, lax.max(below, 0) % 2)
    high_id = (2 * (lax.min(above, slabs - 1) // 2) + side, group, lax.min(above, slabs - 1) % 2)
    has_low, has_high = slab > 0, slab < slabs - 1

    barrier = pltpu.get_barrier_semaphore()

    def greet(i, _):
        g = (group + i) % groups

        @pl.when(jnp.logical_or(jnp.logical_not(has_self), g != group))
        def _():
            pl.semaphore_signal(barrier, inc=1, device_id=(column[0], g, column[1]), device_id_type=MESH)

        return 0

    @pl.when(has_low)
    def _():
        pl.semaphore_signal(barrier, inc=1, device_id=low_id, device_id_type=MESH)

    @pl.when(has_high)
    def _():
        pl.semaphore_signal(barrier, inc=1, device_id=high_id, device_id_type=MESH)

    for i in range(groups):
        greet((i + 1) % groups, 0)

    count = groups - has_self.astype(jnp.int32) + has_low.astype(jnp.int32) + has_high.astype(jnp.int32)
    pl.semaphore_wait(barrier, count)

    keep = pltpu.make_async_copy(lists, lists_both.at[core], list_sems.at[0])
    give = pltpu.make_async_remote_copy(
        src_ref=lists, dst_ref=lists_both.at[core], send_sem=list_sems.at[1], recv_sem=list_sems.at[2],
        device_id=(tile, group, 1 - core), device_id_type=MESH,
    )

    def tabulate():
        def entry(a, s):
            return lists_here[s, TILES * slab + a]

        def slots(a, _):
            for s in range(NBR):
                named = entry(a, s)
                used = named >= 0
                local = lax.min(lax.max(named - TILES * (slab - 1), 0), 3 * TILES - 1)
                places_ref[a * NBR + s] = jnp.where(used, local, TILES + a)
                shares_ref[a * NBR + s] = jnp.where(used, 0.0, 1e30).astype(F32)
            return 0

        def terms(b, _):
            for a in range(TILES):
                slot, share = jnp.int32(0), jnp.float32(0)
                for s in range(NBR):
                    match = entry(a, s) == TILES * (slab - 1) + b
                    slot = jnp.where(match, s, slot)
                    share = jnp.where(match, 1.0, share)
                places_ref[TILES * NBR + b * TILES + a] = a * NBR + slot
                shares_ref[TILES * NBR + b * TILES + a] = share
            return 0

        lax.fori_loop(0, TILES, slots, 0)
        lax.fori_loop(0, 3 * TILES, terms, 0)

    def deliver(src, to, g, sent, landed):
        here = jnp.logical_and(has_self, g == group)

        @pl.when(here)
        def _():
            pltpu.make_async_copy(src, to, landed).start()

        @pl.when(jnp.logical_not(here))
        def _():
            pltpu.make_async_remote_copy(
                src_ref=src, dst_ref=to, send_sem=sent, recv_sem=landed,
                device_id=(column[0], g, column[1]), device_id_type=MESH,
            ).start()

    def spread(*moves):
        def step(i, _):
            for n, (a, j, dst, offset) in enumerate(moves):
                g = (group + i + n * groups // len(moves)) % groups
                src = args[a].at[0, :, pl.ds(pl.multiple_of((g * GROUP + j) * HD, HD), HD)]
                to = dst.at[offset + group * block // TILE, pl.ds(pl.multiple_of(group * block % TILE, block), block), :]
                deliver(src, to, g, send_in.at[a], recv_in.at[a, j])
            return 0

        lax.fori_loop(0, groups, step, 0)

    def arrived(a, j, dst, offset):
        view = dst.at[pl.ds(offset, TILES)]
        pltpu.make_async_copy(view, view, recv_in.at[a, j]).wait()

    def home(*moves):
        def step(i, _):
            for n, (a, j, src) in enumerate(moves):
                g = (group + i + n * groups // len(moves)) % groups
                piece = src.at[g * block // TILE, pl.ds(pl.multiple_of(g * block % TILE, block), block), :]
                to = outs[a].at[0, :, pl.ds(pl.multiple_of((group * GROUP + j) * HD, HD), HD)]
                deliver(piece, to, g, send_out.at[a], recv_out.at[a])
            return 0

        lax.fori_loop(0, groups, step, 0)

    def halo(j, n, direction):
        src = (ks, vs)[n][j]
        return pltpu.make_async_remote_copy(
            src_ref=src.at[pl.ds(TILES, TILES)],
            dst_ref=src.at[pl.ds(0 if direction else 2 * TILES, TILES)],
            send_sem=halo_send.at[j, n, direction], recv_sem=halo_recv.at[j, n, direction],
            device_id=high_id if direction else low_id, device_id_type=MESH,
        )

    def rim(j, n, direction):
        return pltpu.make_async_remote_copy(
            src_ref=rim_out[j][2 * direction + n], dst_ref=rim_in[j][2 * (1 - direction) + n],
            send_sem=rim_send.at[j, n, direction], recv_sem=rim_recv.at[j, n, direction],
            device_id=high_id if direction else low_id, device_id_type=MESH,
        )

    def both(make, j, act):
        for direction in range(2):
            there = (has_low, has_high)[direction]
            source = (has_high, has_low)[direction]
            if act == "start":
                @pl.when(there)
                def _():
                    for n in range(2):
                        make(j, n, direction).start()
            elif act == "recv":
                @pl.when(source)
                def _():
                    for n in range(2):
                        make(j, n, direction).wait_recv()
            else:
                @pl.when(there)
                def _():
                    for n in range(2):
                        make(j, n, direction).wait_send()

    scale = HD ** -0.5
    to_two = scale * math.log2(math.e)

    def attend(j, a):
        starts, hides = [], []
        for s in range(NBR):
            starts.append(places_ref[a * NBR + s])
            hides.append(shares_ref[a * NBR + s])
        q = qs[j][a]
        peak = jnp.full((1, TILE), -1e30, F32)
        for s in range(NBR):
            scores = dot(ks[j][starts[s]], q, NT)
            s_ref[s * TILE:(s + 1) * TILE, :] = scores
            peak = jnp.maximum(peak, jnp.max(scores, axis=0, keepdims=True) - hides[s])
        total = jnp.zeros((1, TILE), F32)
        for s in range(NBR):
            floor = peak + hides[s]
            for c in range(0, TILE, CHUNK):
                part = slice(s * TILE + c, s * TILE + c + CHUNK)
                expo = jnp.exp2((s_ref[part, :] - floor) * to_two)
                total = total + jnp.sum(expo, axis=0, keepdims=True)
                e_ref[part, :] = expo.astype(BF16)
        inverse = 1.0 / total
        g_cols = (gs[j][a].astype(F32).T * inverse).astype(BF16)
        attended = jnp.zeros((HD, TILE), F32)
        delta = jnp.zeros((1, TILE), F32)
        for s in range(NBR):
            v = vs[j][starts[s]]
            span = slice(s * TILE, (s + 1) * TILE)
            s_ref[span, :] = dot(v, g_cols, NN)
            dvc[a * NBR + s] = dot(e_ref[span, :], g_cols, NT)
            attended = attended + dot(v, e_ref[span, :], TN)
            for c in range(0, TILE, CHUNK):
                part = slice(s * TILE + c, s * TILE + c + CHUNK)
                delta = delta + jnp.sum(e_ref[part, :].astype(F32) * s_ref[part, :], axis=0, keepdims=True)
        os[j][a] = (attended * inverse).T.astype(BF16)
        delta = delta * inverse
        grad_q = jnp.zeros((HD, TILE), F32)
        for s in range(NBR):
            for c in range(0, TILE, CHUNK):
                part = slice(s * TILE + c, s * TILE + c + CHUNK)
                d_ref[part, :] = (e_ref[part, :].astype(F32) * (s_ref[part, :] - delta)).astype(BF16)
            span = slice(s * TILE, (s + 1) * TILE)
            dkc[a * NBR + s] = dot(d_ref[span, :], q, NN) * scale
            grad_q = grad_q + dot(ks[j][starts[s]], d_ref[span, :], TN)
        dqs[j][a] = (grad_q * scale).T.astype(BF16)

    def gather(b):
        first = TILES * NBR + b * TILES
        places = [places_ref[first + a] for a in range(TILES)]
        shares = [shares_ref[first + a] for a in range(TILES)]
        k_sum = dkc[places[0]] * shares[0]
        v_sum = dvc[places[0]] * shares[0]
        for a in range(1, TILES):
            k_sum = k_sum + dkc[places[a]] * shares[a]
            v_sum = v_sum + dvc[places[a]] * shares[a]
        return k_sum, v_sum

    def collect(j):
        def lower(i, _):
            k_sum, v_sum = gather(i)
            rim_out[j][0][i] = k_sum.astype(BF16)
            rim_out[j][1][i] = v_sum.astype(BF16)
            return 0

        def upper(i, _):
            k_sum, v_sum = gather(i + 2 * TILES)
            rim_out[j][2][i] = k_sum.astype(BF16)
            rim_out[j][3][i] = v_sum.astype(BF16)
            return 0

        def own(i, _):
            k_sum, v_sum = gather(i + TILES)
            own_k[j][i] = k_sum
            own_v[j][i] = v_sum
            return 0

        lax.fori_loop(0, TILES, lower, 0)
        lax.fori_loop(0, TILES, upper, 0)
        both(rim, j, "start")
        lax.fori_loop(0, TILES, own, 0)

    def combine(j):
        both(rim, j, "recv")

        def step(i, _):
            dks[j][i] = (
                own_k[j][i] + rim_in[j][0][i].astype(F32) + rim_in[j][2][i].astype(F32)
            ).astype(BF16)
            dvs[j][i] = (
                own_v[j][i] + rim_in[j][1][i].astype(F32) + rim_in[j][3][i].astype(F32)
            ).astype(BF16)
            return 0

        lax.fori_loop(0, TILES, step, 0)
        home((2, j, dks[j]), (3, j, dvs[j]))

    for j in range(GROUP):
        spread((1, j, ks[j], TILES), (2, j, vs[j], TILES))
        spread((0, j, qs[j], 0), (3, j, gs[j], 0))
        if j == 0:
            keep.start()
            give.start()

    blank = jnp.zeros((TILES, TILE, HD), BF16)
    for there, first in ((has_low, 0), (has_high, 2)):
        @pl.when(jnp.logical_not(there))
        def _():
            for j in range(GROUP):
                rim_in[j][first][...] = blank
                rim_in[j][first + 1][...] = blank
                ks[j][first * TILES:(first + 1) * TILES] = blank
                vs[j][first * TILES:(first + 1) * TILES] = blank

    keep.wait()
    give.wait()
    down = pltpu.make_async_copy(lists_both.at[side], lists_here, list_sems.at[3])
    down.start()
    down.wait()
    tabulate()

    def pass_on(j):
        arrived(1, j, ks[j], TILES)
        arrived(2, j, vs[j], TILES)
        both(halo, j, "start")

    pass_on(0)
    for j in range(GROUP):
        arrived(0, j, qs[j], 0)
        arrived(3, j, gs[j], 0)
        both(halo, j, "recv")

        def step(a, _):
            attend(j, a)

            @pl.when(a == TILES // 2)
            def _():
                if j < GROUP - 1:
                    pass_on(j + 1)
                if j > 0:
                    combine(j - 1)

            return 0

        lax.fori_loop(0, TILES, step, 0)
        home((0, j, os[j]), (1, j, dqs[j]))
        collect(j)
    combine(GROUP - 1)

    for j in range(GROUP):
        both(halo, j, "send")
        both(rim, j, "send")
    for refs4, sems in ((args, send_in), (outs, send_out)):
        for a in range(4):
            @pl.when(has_self)
            def _():
                view = refs4[a].at[:, :, pl.ds(0, (groups - 1) * GROUP * HD)]
                pltpu.make_async_copy(view, view, sems.at[a]).wait()

            @pl.when(jnp.logical_not(has_self))
            def _():
                pltpu.make_async_copy(refs4[a], refs4[a], sems.at[a]).wait()
    for a in range(4):
        pltpu.make_async_copy(outs[a], outs[a], recv_out.at[a]).wait()


def settle(*refs):
    given, kept, sems = refs[:4], refs[4:8], refs[8]
    parts = sems.shape[1]
    size = given[0].shape[1] // parts
    copies = []
    for i in range(parts):
        for a in range(4):
            rows = pl.ds(i * size, size)
            copies.append(pltpu.make_async_copy(given[a].at[0, rows, :], kept[a].at[0, rows, :], sems.at[a, i]))
    for copy in copies:
        copy.start()
    for copy in copies:
        copy.wait()


def body(queries, keys, values, grad_out, neighbours):
    slabs, groups = lax.axis_size("tile"), lax.axis_size("head")
    rows = TILES * TILE
    lists = neighbours[0].T
    head = pltpu.VMEM((TILES, TILE, HD), BF16)
    wide = pltpu.VMEM((3 * TILES, TILE, HD), BF16)
    total = pltpu.VMEM((TILES, TILE, HD), F32)
    dma = pltpu.SemaphoreType.DMA
    scratch = (
        [head] * (2 * GROUP) + [wide] * (2 * GROUP) + [head] * (4 * GROUP) + [total] * (2 * GROUP)
        + [head] * (8 * GROUP)
        + [
            pltpu.VMEM((NBR * TILE, TILE), F32),
            pltpu.VMEM((NBR * TILE, TILE), BF16),
            pltpu.VMEM((NBR * TILE, TILE), BF16),
            pltpu.VMEM((TILES * NBR, TILE, HD), F32),
            pltpu.VMEM((TILES * NBR, TILE, HD), F32),
            pltpu.VMEM((2,) + lists.shape, jnp.int32),
            pltpu.SMEM(lists.shape, jnp.int32),
            pltpu.SMEM((TILES * NBR + 3 * TILES * TILES,), jnp.int32),
            pltpu.SMEM((TILES * NBR + 3 * TILES * TILES,), F32),
            dma((4,)), dma((4, GROUP)), dma((GROUP, 2, 2)), dma((GROUP, 2, 2)), dma((GROUP, 2, 2)),
            dma((GROUP, 2, 2)), dma((4,)), dma((4,)), dma((4,)),
        ]
    )
    anywhere = pl.BlockSpec(memory_space=pl.ANY)
    shape = jax.ShapeDtypeStruct(queries.shape, BF16)
    results = pl.pallas_call(
        functools.partial(kernel, slabs, groups),
        out_shape=(pltpu.VMEM(queries.shape, BF16),) * 4,
        in_specs=[anywhere] * 5,
        out_specs=(anywhere,) * 4,
        scratch_shapes=scratch,
        compiler_params=pltpu.CompilerParams(
            collective_id=0, has_side_effects=True, vmem_limit_bytes=54 * 1024 * 1024
        ),
    )(*(pltpu.with_memory_space_constraint(x, pltpu.HBM) for x in (queries, keys, values, grad_out)), lists)
    results = [pltpu.with_memory_space_constraint(r, pltpu.VMEM) for r in results]
    return tuple(pl.pallas_call(
        settle,
        out_shape=(shape,) * 4,
        in_specs=[pl.BlockSpec(memory_space=pltpu.VMEM)] * 4,
        out_specs=(anywhere,) * 4,
        scratch_shapes=[dma((4, 1))],
        compiler_params=pltpu.CompilerParams(vmem_limit_bytes=4 * 1024 * 1024),
    )(*results))


def solution(mesh):
    tokens = P("dp", ("tile", "head"), None)
    return jax.shard_map(
        body,
        mesh=mesh,
        in_specs=(tokens,) * 4 + (P("dp", None, None),),
        out_specs=(tokens,) * 4,
        check_vma=False,
    )
```
